768 devices in a mesh: blk: 96 (over z, y_lo, core), owner: 8 (over y_hi, x).
Axes of the slice: x: 4, y: 8 (y_hi: 2, y_lo: 4; y = y_hi * 4 + y_lo), z: 12, core: 2. Of those that a mesh axis runs over, the one named last changes fastest.
Arguments:
- grad_blocks: bfloat16 [2, 6912, 1024], P(None, 'blk', 'owner'), may hold values from -6 to 6
- ginv_factors: bfloat16 [2, 1024, 1024], P(None, None, 'owner'), as said below
- ainv_owned: bfloat16 [8, 6912, 6912], P('owner', 'blk'), as said below
- owner_table: int32 [2], replicated, may hold values from 0 to 7, as said below
- damp_grad: float32 [2], replicated, may hold values from 0.25 to 2
- damp_act: float32 [2], replicated, may hold values from 0.25 to 2
Outputs:
- preconditioned: bfloat16 [2, 6912, 1024], P(None, 'blk', 'owner')
The draws below stay inside these ranges and needn't reach their ends.
Inputs may be any that keep to these rules, and one draw needn't show every extreme that they name: `ginv_factors`: each matrix is symmetric and positive definite. `ainv_owned`: each matrix is symmetric and positive definite. `owner_table`: the layers have distinct owners.
All inputs are finite; a program needn't handle non-finite values.
Results may differ from the reference program's by a relative error of at most 0.0049.
Values may be sent and summed in bfloat16 or wider, within the bound.
No kernel may reach another device: no remote copies, remote signals or barrier semaphores. Data moves between devices by JAX's collectives and lax.ppermute only.
A program may use at most 32 MiB of HBM per device.

```python
import math
import jax
import jax.numpy as jnp
from jax import lax

OUT = 1024
LAYERS = 2
IN = 6912
N_OWNER = 8


def symmetric_factor(noise, diag_key, copies, matrix_order):
    off_diag = (noise + jnp.swapaxes(noise, 1, 2)) * (0.2 / math.sqrt(matrix_order))
    diagonal = jnp.exp(jax.random.uniform(diag_key, (copies, matrix_order), jnp.float32, math.log(0.6), math.log(1.6)))
    identity_mat = jnp.eye(matrix_order, dtype=jnp.float32)
    return off_diag + identity_mat[None, :, :] * diagonal[:, :, None]


def draw_ainv_owned(key, part):
    key = jax.random.fold_in(key, 11)
    noise_key, diag_key = jax.random.split(key)
    noise = jax.random.normal(noise_key, (N_OWNER, IN, IN), jnp.float32)
    return symmetric_factor(noise, diag_key, N_OWNER, IN).astype(jnp.bfloat16)


def draw_ginv_factors(key, part):
    key = jax.random.fold_in(key, 23)
    noise_key, diag_key = jax.random.split(key)
    noise = jax.random.normal(noise_key, (LAYERS, OUT, OUT), jnp.float32)
    return symmetric_factor(noise, diag_key, LAYERS, OUT).astype(jnp.bfloat16)


def draw_owner_table(key, part):
    key = jax.random.fold_in(key, 37)
    pick_key, order_key = jax.random.split(key)
    others = jax.random.permutation(pick_key, jnp.arange(N_OWNER - 1, dtype=jnp.int32))
    chosen = jnp.concatenate([others[:LAYERS - 1], jnp.full((1,), N_OWNER - 1, jnp.int32)])
    return jax.random.permutation(order_key, chosen).astype(jnp.int32)


def block_scale(rng, shape, cuts, low, largest):
    level = 1.0
    for axis_at, shards_of in cuts:
        heights = jax.random.uniform(jax.random.fold_in(jax.random.fold_in(rng, 6), axis_at), (shards_of,), jnp.float32, low / len(cuts), largest / len(cuts))
        level = level * jnp.repeat(jnp.exp(heights), shape[axis_at] // shards_of).reshape((-1,) + (1,) * (len(shape) - 1 - axis_at))
    return level


def scatter_about(rng, dims, deviation, most, cuts=(), kind=jnp.bfloat16):
    values = jax.random.normal(rng, dims, jnp.float32) * deviation
    if len(cuts) > 0:
        values = block_scale(rng, dims, cuts, -0.22, 0.18) * values
    return jnp.clip(values, min=-most, max=most).astype(kind)


def setup_inputs(seed: int = 0) -> dict:
    seeds = jax.random.split(jax.random.key(seed), 7)
    grad_blocks = scatter_about(seeds[0], (LAYERS, IN, OUT), 1.0, 6.0, ((1, 96), (2, 8)))
    ginv_factors = draw_ginv_factors(jax.random.fold_in(seeds[6], 71), 0)
    ainv_owned = draw_ainv_owned(jax.random.fold_in(seeds[6], 71), 0)
    owner_table = draw_owner_table(jax.random.fold_in(seeds[6], 71), 0)
    damp_grad = jnp.clip(jnp.exp(jax.random.uniform(seeds[4], (LAYERS,), jnp.float32, math.log(0.25), math.log(2.0))), 0.25, 2.0)
    damp_act = jnp.clip(jnp.exp(jax.random.uniform(seeds[5], (LAYERS,), jnp.float32, math.log(0.25), math.log(2.0))), 0.25, 2.0)
    return dict(grad_blocks=grad_blocks, ginv_factors=ginv_factors, ainv_owned=ainv_owned, owner_table=owner_table, damp_grad=damp_grad, damp_act=damp_act)


def reference(grad_blocks, ginv_factors, ainv_owned, owner_table, damp_grad, damp_act):
    results = []
    for layer_index in range(LAYERS):
        gradient = grad_blocks[layer_index]
        right_side = jnp.dot(gradient, ginv_factors[layer_index], preferred_element_type=jnp.float32)
        right_side = (right_side + damp_grad[layer_index] * gradient.astype(jnp.float32)).astype(jnp.bfloat16)
        factor_now = lax.dynamic_index_in_dim(ainv_owned, owner_table[layer_index].astype(jnp.int32), 0, keepdims=False)
        left_side = jnp.dot(factor_now, right_side, preferred_element_type=jnp.float32)
        left_side = left_side + damp_act[layer_index] * right_side.astype(jnp.float32)
        results.append(left_side.astype(jnp.bfloat16))
    return jnp.stack(results)
```

```python
import numpy as np
import jax
import jax.numpy as jnp
from jax import lax
from jax.sharding import Mesh, PartitionSpec as P

LAYERS = 2
AXES = ("z", "ylo", "core", "yhi", "x")
SIZES = (12, 4, 2, 2, 4)
NZ, NY, NC, NH, NX = SIZES
BLK = ("z", "ylo", "core")
OWNER = ("yhi", "x")
CHUNK = ("ylo", "x")
N_CHUNK = NY * NX
BLOCKS = NZ * NY * NC // N_CHUNK


def flat(z, ylo, core, yhi, x):
    return int(np.ravel_multi_index((z, ylo, core, yhi, x), SIZES))


def spread_pairs():
    pairs = []
    for z, ylo, core, yhi, x in np.ndindex(*SIZES):
        block = (z * NY + ylo) * NC + core
        chunk, part = divmod(block, BLOCKS)
        to_core, to_z = divmod(part * NX + x, NZ)
        to_ylo, to_x = divmod(chunk, NX)
        pairs.append((flat(z, ylo, core, yhi, x), flat(to_z, to_ylo, to_core, yhi, to_x)))
    return pairs


def copies(value, axis, count):
    return lax.all_to_all(jnp.broadcast_to(value[None], (count,) + value.shape), axis, 0, 0)


def body(grad_blocks, ginv_factors, ainv_owned, owner_table, damp_grad, damp_act):
    rows, cols = grad_blocks.shape[1:]
    width = ainv_owned.shape[2] // N_CHUNK
    yhi = lax.axis_index("yhi")
    core = lax.axis_index("core")

    gathered = copies(grad_blocks, OWNER, NH * NX)
    gathered = gathered.transpose(1, 2, 0, 3).reshape(LAYERS, rows, NH * NX * cols)
    right = lax.dot_general(
        gathered, ginv_factors, (((2,), (1,)), ((0,), (0,))), preferred_element_type=jnp.float32
    )
    right = right + damp_grad[:, None, None] * grad_blocks.astype(jnp.float32)
    right = right.astype(jnp.bfloat16)

    factor = ainv_owned[0].reshape(rows, N_CHUNK, width).transpose(1, 0, 2)
    factor = lax.all_to_all(factor, CHUNK, 0, 0).reshape(NY, NX, rows, width)
    owner_half = owner_table // NX
    mine = jnp.stack(
        [
            lax.dynamic_index_in_dim(factor, owner_table[l] % NX, 1, keepdims=False)
            for l in range(LAYERS)
        ]
    ).reshape(LAYERS, NY * rows, width)
    other = lax.ppermute(mine, "yhi", [(0, 1), (1, 0)])
    factor = jnp.where((owner_half == yhi)[:, None, None], mine, other)

    piece = lax.ppermute(right, AXES, spread_pairs())
    along_z = copies(piece, "z", NZ)
    swapped = lax.ppermute(along_z, "core", [(0, 1), (1, 0)])
    first = jnp.where(core == 0, along_z, swapped)
    second = jnp.where(core == 0, swapped, along_z)
    chunk = jnp.stack([first, second]).reshape(BLOCKS, NX, LAYERS, rows, cols)
    chunk = chunk.transpose(2, 0, 3, 1, 4).reshape(LAYERS, BLOCKS * rows, NX * cols)

    partial = lax.dot_general(
        factor, chunk, (((2,), (1,)), ((0,), (0,))), preferred_element_type=jnp.float32
    )
    partial = partial.reshape(LAYERS, NY, rows, NX, cols).transpose(1, 3, 0, 2, 4)
    partial = partial.reshape(N_CHUNK, LAYERS, rows, cols)
    act = jnp.sum(lax.all_to_all(partial, CHUNK, 0, 0), axis=0)
    act = act + damp_act[:, None, None] * right.astype(jnp.float32)
    return act.astype(jnp.bfloat16)


def solution(mesh):
    fine = Mesh(mesh.devices.reshape(SIZES), AXES)
    return jax.shard_map(
        body,
        mesh=fine,
        in_specs=(
            P(None, BLK, OWNER),
            P(None, None, OWNER),
            P(OWNER, BLK, None),
            P(),
            P(),
            P(),
        ),
        out_specs=P(None, BLK, OWNER),
        check_vma=False,
    )
```

```python
import numpy as np
import jax
import jax.numpy as jnp
from jax import lax
from jax.sharding import Mesh, PartitionSpec as P

LAYERS = 2
AXES = ("za", "zb", "ya", "yb", "core", "yhi", "x")
SIZES = (6, 2, 2, 2, 2, 2, 4)
NX = 4
N_OWNER = 8
BLK = ("za", "zb", "ya", "yb", "core")
OWNER = ("yhi", "x")
CHUNK = ("zb", "yb", "x")
MEMBERS = ("za", "ya")
N_CHUNK = 16
N_ROWS = 4
BLOCKS = 6
N_MEMBER = 12


def flat(*index):
    return int(np.ravel_multi_index(index, SIZES))


def spread_pairs():
    pairs = []
    for index in np.ndindex(*SIZES):
        block = int(np.ravel_multi_index(index[:5], SIZES[:5]))
        yhi, x = index[5:]
        chunk, part = divmod(block, BLOCKS)
        to_core, member = divmod(part * NX + x, N_MEMBER)
        to_za, to_ya = divmod(member, 2)
        to_zb, to_yb, to_x = np.unravel_index(chunk, (2, 2, NX))
        pairs.append((flat(*index), flat(to_za, to_zb, to_ya, to_yb, to_core, yhi, to_x)))
    return pairs


def copies(value, axis, count):
    return lax.all_to_all(jnp.broadcast_to(value[None], (count,) + value.shape), axis, 0, 0)


def body(grad_blocks, ginv_factors, ainv_owned, owner_table, damp_grad, damp_act):
    rows, cols = grad_blocks.shape[1:]
    width = ainv_owned.shape[2] // N_CHUNK
    yhi = lax.axis_index("yhi")
    core = lax.axis_index("core")

    factor = ainv_owned[0].reshape(rows, N_CHUNK, width).transpose(1, 0, 2)
    factor = lax.all_to_all(factor, CHUNK, 0, 0).reshape(N_ROWS, NX, rows, width)
    owner_half = owner_table // NX
    mine = jnp.stack(
        [
            lax.dynamic_index_in_dim(factor, owner_table[l] % NX, 1, keepdims=False)
            for l in range(LAYERS)
        ]
    ).reshape(LAYERS, N_ROWS * rows, width)
    mine, gradient = lax.optimization_barrier((mine, grad_blocks))
    other = lax.ppermute(mine, "yhi", [(0, 1), (1, 0)])

    gathered = copies(gradient, OWNER, N_OWNER)
    gathered = gathered.transpose(1, 2, 0, 3).reshape(LAYERS, rows, N_OWNER * cols)
    right = lax.dot_general(
        gathered, ginv_factors, (((2,), (1,)), ((0,), (0,))), preferred_element_type=jnp.float32
    )
    right = right + damp_grad[:, None, None] * grad_blocks.astype(jnp.float32)
    right = right.astype(jnp.bfloat16)
    piece = lax.ppermute(right, AXES, spread_pairs())
    other, piece = lax.optimization_barrier((other, piece))
    factor = jnp.where((owner_half == yhi)[:, None, None], mine, other)

    along_z = copies(piece, MEMBERS, N_MEMBER)
    swapped = lax.ppermute(along_z, "core", [(0, 1), (1, 0)])
    first = jnp.where(core == 0, along_z, swapped)
    second = jnp.where(core == 0, swapped, along_z)
    chunk = jnp.stack([first, second]).reshape(BLOCKS, NX, LAYERS, rows, cols)
    chunk = chunk.transpose(2, 0, 3, 1, 4).reshape(LAYERS, BLOCKS * rows, NX * cols)

    partial = lax.dot_general(
        factor, chunk, (((2,), (1,)), ((0,), (0,))), preferred_element_type=jnp.float32
    )
    partial = partial.reshape(LAYERS, N_ROWS, rows, NX, cols).transpose(1, 3, 0, 2, 4)
    partial = partial.reshape(N_CHUNK, LAYERS, rows, cols)
    act = jnp.sum(lax.all_to_all(partial, CHUNK, 0, 0), axis=0)
    act = act + damp_act[:, None, None] * right.astype(jnp.float32)
    return act.astype(jnp.bfloat16)


def solution(mesh):
    fine = Mesh(mesh.devices.reshape(SIZES), AXES)
    return jax.shard_map(
        body,
        mesh=fine,
        in_specs=(
            P(None, BLK, OWNER),
            P(None, None, OWNER),
            P(OWNER, BLK, None),
            P(),
            P(),
            P(),
        ),
        out_specs=P(None, BLK, OWNER),
        check_vma=False,
    )
```

```python
import numpy as np
import jax
import jax.numpy as jnp
from jax import lax
from jax.experimental import pallas as pl
from jax.sharding import Mesh, PartitionSpec as P

LAYERS = 2
AXES = ("za", "zb", "ya", "yb", "core", "yhi", "x")
SIZES = (6, 2, 2, 2, 2, 2, 4)
NX = 4
N_OWNER = 8
BLK = ("za", "zb", "ya", "yb", "core")
OWNER = ("yhi", "x")
CHUNK = ("zb", "yb", "x")
N_CHUNK = 16
N_ROWS = 4
BLOCKS = 6
FLIP = [(0, 1), (1, 0)]


def spread_pairs(flip):
    source = np.arange(np.prod(SIZES)).reshape(SIZES)
    pairs = []
    for za, zb, ya, yb, core, yhi, x in np.ndindex(*SIZES):
        target = source[za, zb, (x // 2) ^ flip, yb, x % 2, yhi, 2 * ya + core]
        pairs.append((int(source[za, zb, ya, yb, core, yhi, x]), int(target)))
    return pairs


def copies(value, axis, count):
    return lax.all_to_all(jnp.broadcast_to(value[None], (count,) + value.shape), axis, 0, 0)


def ordered(mine, other, axis):
    first = lax.axis_index(axis) == 0
    return jnp.stack([jnp.where(first, mine, other), jnp.where(first, other, mine)])


def chunk_kernel(factor_ref, chunks_ref):
    rows = factor_ref.shape[1]
    for zb, yb, ya, core in np.ndindex(2, 2, 2, 2):
        at = ((zb * 2 + ya) * 2 + yb) * 2 + core
        runs = [
            factor_ref[0, :, (za * N_CHUNK + at) * rows : (za * N_CHUNK + at + 1) * rows]
            for za in range(BLOCKS)
        ]
        chunks_ref[((zb * 2 + yb) * 2 + ya) * 2 + core] = jnp.concatenate(runs, axis=1)


def column_chunks(factor):
    _, rows, width = factor.shape
    return pl.pallas_call(
        chunk_kernel,
        out_shape=jax.ShapeDtypeStruct((N_CHUNK, rows, width // N_CHUNK), factor.dtype),
        cost_estimate=pl.CostEstimate(
            flops=0, bytes_accessed=4 * rows * width, transcendentals=0
        ),
    )(factor)


def body(grad_blocks, ginv_factors, ainv_owned, owner_table, damp_grad, damp_act):
    rows, cols = grad_blocks.shape[1:]
    width = ainv_owned.shape[2] // N_CHUNK
    yhi = lax.axis_index("yhi")

    gathered = copies(grad_blocks, OWNER, N_OWNER)
    gathered = gathered.transpose(1, 2, 0, 3).reshape(LAYERS, rows, N_OWNER * cols)
    right = lax.dot_general(
        gathered, ginv_factors, (((2,), (1,)), ((0,), (0,))), preferred_element_type=jnp.float32
    )
    right = right + damp_grad[:, None, None] * grad_blocks.astype(jnp.float32)
    right = right.astype(jnp.bfloat16)
    near = lax.ppermute(right, AXES, spread_pairs(0))
    far = lax.ppermute(right, AXES, spread_pairs(1))
    piece = ordered(near, far, "ya")

    factor = column_chunks(ainv_owned)
    factor = lax.all_to_all(factor, CHUNK, 0, 0).reshape(N_ROWS, NX, rows, width)
    owner_half = owner_table // NX
    mine = jnp.stack(
        [
            lax.dynamic_index_in_dim(factor, owner_table[l] % NX, 1, keepdims=False)
            for l in range(LAYERS)
        ]
    ).reshape(LAYERS, N_ROWS * rows, width)
    mine, piece = lax.optimization_barrier((mine, piece))
    other = lax.ppermute(mine, "yhi", FLIP)

    along = copies(piece, "za", BLOCKS)
    along, other = lax.optimization_barrier((along, other))
    factor = jnp.where((owner_half == yhi)[:, None, None], mine, other)
    chunk = ordered(along, lax.ppermute(along, "core", FLIP), "core")
    chunk = chunk.transpose(3, 1, 4, 2, 0, 5).reshape(LAYERS, BLOCKS * rows, NX * cols)

    partial = lax.dot_general(
        factor, chunk, (((2,), (1,)), ((0,), (0,))), preferred_element_type=jnp.float32
    )
    partial = partial.reshape(LAYERS, N_ROWS, rows, NX, cols).transpose(1, 3, 0, 2, 4)
    partial = partial.reshape(N_CHUNK, LAYERS, rows, cols)
    act = jnp.sum(lax.all_to_all(partial, CHUNK, 0, 0), axis=0)
    act = act + damp_act[:, None, None] * right.astype(jnp.float32)
    return act.astype(jnp.bfloat16)


def solution(mesh):
    fine = Mesh(mesh.devices.reshape(SIZES), AXES)
    return jax.shard_map(
        body,
        mesh=fine,
        in_specs=(
            P(None, BLK, OWNER),
            P(None, None, OWNER),
            P(OWNER, BLK, None),
            P(),
            P(),
            P(),
        ),
        out_specs=P(None, BLK, OWNER),
        check_vma=False,
    )
```

```python
import numpy as np
import jax
import jax.numpy as jnp
from jax import lax
from jax.experimental import pallas as pl
from jax.sharding import Mesh, PartitionSpec as P

LAYERS = 2
AXES = ("za", "zb", "ya", "yb", "core", "yhi", "x")
SIZES = (6, 2, 2, 2, 2, 2, 4)
NX = 4
N_OWNER = 8
BLK = ("za", "zb", "ya", "yb", "core")
OWNER = ("yhi", "x")
CHUNK = ("zb", "yb", "x")
N_CHUNK = 16
N_ROWS = 4
BLOCKS = 6
FLIP = [(0, 1), (1, 0)]


def spread_pairs(flip):
    source = np.arange(np.prod(SIZES)).reshape(SIZES)
    pairs = []
    for za, zb, ya, yb, core, yhi, x in np.ndindex(*SIZES):
        target = source[za, zb, (x // 2) ^ flip, yb, x % 2, yhi, 2 * ya + core]
        pairs.append((int(source[za, zb, ya, yb, core, yhi, x]), int(target)))
    return pairs


def copies(value, axis, count):
    return lax.all_to_all(jnp.broadcast_to(value[None], (count,) + value.shape), axis, 0, 0)


def ordered(mine, other, axis):
    first = lax.axis_index(axis) == 0
    return jnp.stack([jnp.where(first, mine, other), jnp.where(first, other, mine)])


def chunk_kernel(factor_ref, chunks_ref):
    rows = factor_ref.shape[1]
    for zb, yb, ya, core in np.ndindex(2, 2, 2, 2):
        at = ((zb * 2 + ya) * 2 + yb) * 2 + core
        runs = [
            factor_ref[0, :, (za * N_CHUNK + at) * rows : (za * N_CHUNK + at + 1) * rows]
            for za in range(BLOCKS)
        ]
        chunks_ref[((zb * 2 + yb) * 2 + ya) * 2 + core] = jnp.concatenate(runs, axis=1)


def column_chunks(factor):
    _, rows, width = factor.shape
    return pl.pallas_call(
        chunk_kernel,
        out_shape=jax.ShapeDtypeStruct((N_CHUNK, rows, width // N_CHUNK), factor.dtype),
        cost_estimate=pl.CostEstimate(
            flops=0, bytes_accessed=4 * rows * width, transcendentals=0
        ),
    )(factor)


def body(grad_blocks, ginv_factors, ainv_owned, owner_table, damp_grad, damp_act):
    rows, cols = grad_blocks.shape[1:]
    width = ainv_owned.shape[2] // N_CHUNK
    yhi = lax.axis_index("yhi")

    gathered = copies(grad_blocks, OWNER, N_OWNER)
    gathered = gathered.transpose(1, 2, 0, 3).reshape(LAYERS, rows, N_OWNER * cols)
    right = lax.dot_general(
        gathered, ginv_factors, (((2,), (1,)), ((0,), (0,))), preferred_element_type=jnp.float32
    )
    right = right + damp_grad[:, None, None] * grad_blocks.astype(jnp.float32)
    right = right.astype(jnp.bfloat16)
    near = lax.ppermute(right, AXES, spread_pairs(0))
    far = lax.ppermute(right, AXES, spread_pairs(1))
    piece = ordered(near, far, "ya")

    factor = column_chunks(ainv_owned)
    factor = lax.all_to_all(factor, CHUNK, 0, 0).reshape(N_ROWS, NX, rows, width)
    owner_half = owner_table // NX
    here = owner_half == yhi

    def of_owner(owner):
        part = lax.dynamic_index_in_dim(factor, owner % NX, 1, keepdims=False)
        return part.reshape(N_ROWS * rows, width)

    mine = [of_owner(owner_table[l]) for l in range(LAYERS)]
    one_half = owner_half[0] == owner_half[1]
    first = of_owner(jnp.where(here[0], owner_table[0], owner_table[1]))
    first, piece = lax.optimization_barrier((first, piece))
    first = lax.ppermute(first, "yhi", FLIP)
    second = lax.cond(one_half, lambda part: lax.ppermute(part, "yhi", FLIP), lambda part: part, mine[1])

    along = copies(piece, "za", BLOCKS)
    along, first = lax.optimization_barrier((along, first))
    factor = jnp.stack(
        [
            jnp.where(here[0], mine[0], first),
            jnp.where(here[1], mine[1], jnp.where(one_half, second, first)),
        ]
    )
    chunk = ordered(along, lax.ppermute(along, "core", FLIP), "core")
    chunk = chunk.transpose(3, 1, 4, 2, 0, 5).reshape(LAYERS, BLOCKS * rows, NX * cols)

    partial = lax.dot_general(
        factor, chunk, (((2,), (1,)), ((0,), (0,))), preferred_element_type=jnp.float32
    )
    partial = partial.reshape(LAYERS, N_ROWS, rows, NX, cols).transpose(1, 3, 0, 2, 4)
    partial = partial.reshape(N_CHUNK, LAYERS, rows, cols)
    act = jnp.sum(lax.all_to_all(partial, CHUNK, 0, 0), axis=0)
    act = act + damp_act[:, None, None] * right.astype(jnp.float32)
    return act.astype(jnp.bfloat16)


def solution(mesh):
    fine = Mesh(mesh.devices.reshape(SIZES), AXES)
    return jax.shard_map(
        body,
        mesh=fine,
        in_specs=(
            P(None, BLK, OWNER),
            P(None, None, OWNER),
            P(OWNER, BLK, None),
            P(),
            P(),
            P(),
        ),
        out_specs=P(None, BLK, OWNER),
        check_vma=False,
    )
```

```python
import numpy as np
import jax
import jax.numpy as jnp
from jax import lax
from jax.experimental import pallas as pl
from jax.sharding import Mesh, PartitionSpec as P

LAYERS = 2
AXES = ("za", "zb", "ya", "yb", "core", "yhi", "x")
SIZES = (6, 2, 2, 2, 2, 2, 4)
NX = 4
N_OWNER = 8
BLK = ("za", "zb", "ya", "yb", "core")
OWNER = ("yhi", "x")
CHUNK = ("zb", "yb", "x")
N_CHUNK = 16
N_ROWS = 4
BLOCKS = 6
FLIP = [(0, 1), (1, 0)]


def spread_pairs(flip):
    source = np.arange(np.prod(SIZES)).reshape(SIZES)
    pairs = []
    for za, zb, ya, yb, core, yhi, x in np.ndindex(*SIZES):
        target = source[za, zb, (x // 2) ^ flip, yb, x % 2, yhi, 2 * ya + core]
        pairs.append((int(source[za, zb, ya, yb, core, yhi, x]), int(target)))
    return pairs


def copies(value, axis, count):
    return lax.all_to_all(jnp.broadcast_to(value[None], (count,) + value.shape), axis, 0, 0)


def ordered(mine, other, axis):
    first = lax.axis_index(axis) == 0
    return jnp.stack([jnp.where(first, mine, other), jnp.where(first, other, mine)])


def chunk_kernel(factor_ref, chunks_ref):
    rows = factor_ref.shape[1]
    for zb, yb, ya, core in np.ndindex(2, 2, 2, 2):
        at = ((zb * 2 + ya) * 2 + yb) * 2 + core
        runs = [
            factor_ref[0, :, (za * N_CHUNK + at) * rows : (za * N_CHUNK + at + 1) * rows]
            for za in range(BLOCKS)
        ]
        chunks_ref[((zb * 2 + yb) * 2 + ya) * 2 + core] = jnp.concatenate(runs, axis=1)


def column_chunks(factor):
    _, rows, width = factor.shape
    return pl.pallas_call(
        chunk_kernel,
        out_shape=jax.ShapeDtypeStruct((N_CHUNK, rows, width // N_CHUNK), factor.dtype),
        cost_estimate=pl.CostEstimate(
            flops=0, bytes_accessed=4 * rows * width, transcendentals=0
        ),
    )(factor)


def body(grad_blocks, ginv_factors, ainv_owned, owner_table, damp_grad, damp_act):
    rows, cols = grad_blocks.shape[1:]
    width = ainv_owned.shape[2] // N_CHUNK
    yhi = lax.axis_index("yhi")

    gathered = copies(grad_blocks, OWNER, N_OWNER)
    gathered = gathered.transpose(1, 2, 0, 3).reshape(LAYERS, rows, N_OWNER * cols)
    right = lax.dot_general(
        gathered, ginv_factors, (((2,), (1,)), ((0,), (0,))), preferred_element_type=jnp.float32
    )
    right = right + damp_grad[:, None, None] * grad_blocks.astype(jnp.float32)
    right = right.astype(jnp.bfloat16)
    near = lax.ppermute(right, AXES, spread_pairs(0))
    far = lax.ppermute(right, AXES, spread_pairs(1))
    piece = ordered(near, far, "ya")

    factor = column_chunks(ainv_owned)
    factor = lax.all_to_all(factor, CHUNK, 0, 0).reshape(N_ROWS, NX, rows, width)
    owner_half = owner_table // NX
    here = owner_half == yhi

    def of_owner(owner):
        part = lax.dynamic_index_in_dim(factor, owner % NX, 1, keepdims=False)
        return part.reshape(N_ROWS * rows, width)

    mine = [of_owner(owner_table[l]) for l in range(LAYERS)]
    one_half = owner_half[0] == owner_half[1]
    first = of_owner(jnp.where(here[0], owner_table[0], owner_table[1]))
    first, piece = lax.optimization_barrier((first, piece))
    first = lax.ppermute(first, "yhi", FLIP)
    second = lax.cond(one_half, lambda part: lax.ppermute(part, "yhi", FLIP), lambda part: part, mine[1])

    along = copies(piece, "za", BLOCKS)
    along, first = lax.optimization_barrier((along, first))
    factor = jnp.stack(
        [
            jnp.where(here[0], mine[0], first),
            jnp.where(here[1], mine[1], jnp.where(one_half, second, first)),
        ]
    )
    chunk = ordered(along, lax.ppermute(along, "core", FLIP), "core")
    chunk = chunk.transpose(3, 1, 4, 2, 0, 5).reshape(LAYERS, BLOCKS * rows, NX * cols)

    partial = lax.dot_general(
        factor, chunk, (((2,), (1,)), ((0,), (0,))), preferred_element_type=jnp.float32
    )
    partial = partial.reshape(LAYERS, N_ROWS, rows, NX, cols).transpose(1, 3, 0, 2, 4)
    partial = partial.reshape(N_CHUNK, LAYERS, rows, cols).astype(jnp.bfloat16)
    act = jnp.sum(lax.all_to_all(partial, CHUNK, 0, 0).astype(jnp.float32), axis=0)
    act = act + damp_act[:, None, None] * right.astype(jnp.float32)
    return act.astype(jnp.bfloat16)


def solution(mesh):
    fine = Mesh(mesh.devices.reshape(SIZES), AXES)
    return jax.shard_map(
        body,
        mesh=fine,
        in_specs=(
            P(None, BLK, OWNER),
            P(None, None, OWNER),
            P(OWNER, BLK, None),
            P(),
            P(),
            P(),
        ),
        out_specs=P(None, BLK, OWNER),
        check_vma=False,
    )
```

```python
import numpy as np
import jax
import jax.numpy as jnp
from jax import lax
from jax.experimental import pallas as pl
from jax.sharding import Mesh, PartitionSpec as P

LAYERS = 2
AXES = ("za", "zb", "ya", "yb", "core", "yhi", "x")
SIZES = (6, 2, 2, 2, 2, 2, 4)
NX = 4
N_OWNER = 8
BLK = ("za", "zb", "ya", "yb", "core")
OWNER = ("yhi", "x")
CHUNK = ("zb", "yb", "x")
N_CHUNK = 16
N_ROWS = 4
BLOCKS = 6
FLIP = [(0, 1), (1, 0)]


def spread_pairs(flip):
    source = np.arange(np.prod(SIZES)).reshape(SIZES)
    pairs = []
    for za, zb, ya, yb, core, yhi, x in np.ndindex(*SIZES):
        target = source[za, zb, (x // 2) ^ flip, yb, x % 2, yhi, 2 * ya + core]
        pairs.append((int(source[za, zb, ya, yb, core, yhi, x]), int(target)))
    return pairs


def copies(value, axis, count):
    return lax.all_to_all(jnp.broadcast_to(value[None], (count,) + value.shape), axis, 0, 0)


def ordered(mine, other, axis):
    first = lax.axis_index(axis) == 0
    return jnp.stack([jnp.where(first, mine, other), jnp.where(first, other, mine)])


def chunk_kernel(factor_ref, chunks_ref):
    rows = factor_ref.shape[1]
    for zb, yb, ya, core in np.ndindex(2, 2, 2, 2):
        at = ((zb * 2 + ya) * 2 + yb) * 2 + core
        runs = [
            factor_ref[0, :, (za * N_CHUNK + at) * rows : (za * N_CHUNK + at + 1) * rows]
            for za in range(BLOCKS)
        ]
        chunks_ref[((zb * 2 + yb) * 2 + ya) * 2 + core] = jnp.concatenate(runs, axis=1)


def column_chunks(factor):
    _, rows, width = factor.shape
    return pl.pallas_call(
        chunk_kernel,
        out_shape=jax.ShapeDtypeStruct((N_CHUNK, rows, width // N_CHUNK), factor.dtype),
        cost_estimate=pl.CostEstimate(
            flops=0, bytes_accessed=4 * rows * width, transcendentals=0
        ),
    )(factor)


def body(grad_blocks, ginv_factors, ainv_owned, owner_table, damp_grad, damp_act):
    rows, cols = grad_blocks.shape[1:]
    width = ainv_owned.shape[2] // N_CHUNK
    yhi = lax.axis_index("yhi")

    gathered = copies(grad_blocks, OWNER, N_OWNER)
    gathered = gathered.transpose(1, 2, 0, 3).reshape(LAYERS, rows, N_OWNER * cols)
    right = lax.dot_general(
        gathered, ginv_factors, (((2,), (1,)), ((0,), (0,))), preferred_element_type=jnp.float32
    )
    right = right + damp_grad[:, None, None] * grad_blocks.astype(jnp.float32)
    right = right.astype(jnp.bfloat16)
    near = lax.ppermute(right, AXES, spread_pairs(0))
    far = lax.ppermute(right, AXES, spread_pairs(1))
    piece = ordered(near, far, "ya")

    factor = column_chunks(ainv_owned)
    factor = lax.all_to_all(factor, CHUNK, 0, 0).reshape(N_ROWS, NX, rows, width)
    owner_half = owner_table // NX
    here = owner_half == yhi

    def of_owner(owner):
        part = lax.dynamic_index_in_dim(factor, owner % NX, 1, keepdims=False)
        return part.reshape(N_ROWS * rows, width)

    mine = [of_owner(owner_table[l]) for l in range(LAYERS)]
    one_half = owner_half[0] == owner_half[1]
    first = of_owner(jnp.where(here[0], owner_table[0], owner_table[1]))
    first = lax.ppermute(first, "yhi", FLIP)
    second = lax.cond(one_half, lambda part: lax.ppermute(part, "yhi", FLIP), lambda part: part, mine[1])

    za = lax.axis_index("za")
    along = jnp.zeros((BLOCKS,) + piece.shape, piece.dtype)
    for step in range(BLOCKS):
        ahead = [((at + step) % BLOCKS, at) for at in range(BLOCKS)]
        block = lax.ppermute(piece, "za", ahead) if step else piece
        along = lax.dynamic_update_index_in_dim(along, block, (za + step) % BLOCKS, 0)
    along, first, second = lax.optimization_barrier((along, first, second))
    factor = jnp.stack(
        [
            jnp.where(here[0], mine[0], first),
            jnp.where(here[1], mine[1], jnp.where(one_half, second, first)),
        ]
    )
    chunk = ordered(along, lax.ppermute(along, "core", FLIP), "core")
    chunk = chunk.transpose(3, 1, 4, 2, 0, 5).reshape(LAYERS, BLOCKS * rows, NX * cols)

    partial = lax.dot_general(
        factor, chunk, (((2,), (1,)), ((0,), (0,))), preferred_element_type=jnp.float32
    )
    partial = partial.reshape(LAYERS, N_ROWS, rows, NX, cols).transpose(1, 3, 0, 2, 4)
    partial = partial.reshape(N_CHUNK, LAYERS, rows, cols)
    act = jnp.sum(lax.all_to_all(partial, CHUNK, 0, 0), axis=0)
    act = act + damp_act[:, None, None] * right.astype(jnp.float32)
    return act.astype(jnp.bfloat16)


def solution(mesh):
    fine = Mesh(mesh.devices.reshape(SIZES), AXES)
    return jax.shard_map(
        body,
        mesh=fine,
        in_specs=(
            P(None, BLK, OWNER),
            P(None, None, OWNER),
            P(OWNER, BLK, None),
            P(),
            P(),
            P(),
        ),
        out_specs=P(None, BLK, OWNER),
        check_vma=False,
    )
```

```python
import numpy as np
import jax
import jax.numpy as jnp
from jax import lax
from jax.experimental import pallas as pl
from jax.sharding import Mesh, PartitionSpec as P

LAYERS = 2
AXES = ("za", "zb", "ya", "yb", "core", "yhi", "x")
SIZES = (6, 2, 2, 2, 2, 2, 4)
NX = 4
N_OWNER = 8
BLK = ("za", "zb", "ya", "yb", "core")
OWNER = ("yhi", "x")
CHUNK = ("zb", "yb", "x")
N_CHUNK = 16
N_ROWS = 4
BLOCKS = 6
FLIP = [(0, 1), (1, 0)]


def spread_pairs(flip):
    source = np.arange(np.prod(SIZES)).reshape(SIZES)
    pairs = []
    for za, zb, ya, yb, core, yhi, x in np.ndindex(*SIZES):
        target = source[za, zb, (x // 2) ^ flip, yb, x % 2, yhi, 2 * ya + core]
        pairs.append((int(source[za, zb, ya, yb, core, yhi, x]), int(target)))
    return pairs


def copies(value, axis, count):
    return lax.all_to_all(jnp.broadcast_to(value[None], (count,) + value.shape), axis, 0, 0)


def ordered(mine, other, axis):
    first = lax.axis_index(axis) == 0
    return jnp.stack([jnp.where(first, mine, other), jnp.where(first, other, mine)])


def chunk_kernel(factor_ref, chunks_ref):
    rows = factor_ref.shape[1]
    for zb, yb, ya, core in np.ndindex(2, 2, 2, 2):
        at = ((zb * 2 + ya) * 2 + yb) * 2 + core
        runs = [
            factor_ref[0, :, (za * N_CHUNK + at) * rows : (za * N_CHUNK + at + 1) * rows]
            for za in range(BLOCKS)
        ]
        chunks_ref[((zb * 2 + yb) * 2 + ya) * 2 + core] = jnp.concatenate(runs, axis=1)


def column_chunks(factor):
    _, rows, width = factor.shape
    return pl.pallas_call(
        chunk_kernel,
        out_shape=jax.ShapeDtypeStruct((N_CHUNK, rows, width // N_CHUNK), factor.dtype),
        cost_estimate=pl.CostEstimate(
            flops=0, bytes_accessed=4 * rows * width, transcendentals=0
        ),
    )(factor)


def body(grad_blocks, ginv_factors, ainv_owned, owner_table, damp_grad, damp_act):
    rows, cols = grad_blocks.shape[1:]
    width = ainv_owned.shape[2] // N_CHUNK
    yhi = lax.axis_index("yhi")

    gathered = copies(grad_blocks, OWNER, N_OWNER)
    gathered = gathered.transpose(1, 2, 0, 3).reshape(LAYERS, rows, N_OWNER * cols)
    right = lax.dot_general(
        gathered, ginv_factors, (((2,), (1,)), ((0,), (0,))), preferred_element_type=jnp.float32
    )
    right = right + damp_grad[:, None, None] * grad_blocks.astype(jnp.float32)
    right = right.astype(jnp.bfloat16)
    near = lax.ppermute(right, AXES, spread_pairs(0))
    far = lax.ppermute(right, AXES, spread_pairs(1))
    piece = ordered(near, far, "ya")

    factor = column_chunks(ainv_owned)
    factor = lax.all_to_all(factor, CHUNK, 0, 0).reshape(N_ROWS, NX, rows, width)
    owner_half = owner_table // NX
    here = owner_half == yhi

    def of_owner(owner):
        part = lax.dynamic_index_in_dim(factor, owner % NX, 1, keepdims=False)
        return part.reshape(N_ROWS * rows, width)

    mine = [of_owner(owner_table[l]) for l in range(LAYERS)]
    one_half = owner_half[0] == owner_half[1]
    first = of_owner(jnp.where(here[0], owner_table[0], owner_table[1]))
    first, piece = lax.optimization_barrier((first, piece))
    first = lax.ppermute(first, "yhi", FLIP)
    second = lax.cond(one_half, lambda part: lax.ppermute(part, "yhi", FLIP), lambda part: part, mine[1])

    along = copies(piece, "za", BLOCKS)
    along, first, second = lax.optimization_barrier((along, first, second))
    factor = jnp.stack(
        [
            jnp.where(here[0], mine[0], first),
            jnp.where(here[1], mine[1], jnp.where(one_half, second, first)),
        ]
    )
    chunk = ordered(along, lax.ppermute(along, "core", FLIP), "core")
    chunk = chunk.transpose(3, 1, 4, 2, 0, 5).reshape(LAYERS, BLOCKS * rows, NX * cols)

    partial = lax.dot_general(
        factor, chunk, (((2,), (1,)), ((0,), (0,))), preferred_element_type=jnp.float32
    )
    partial = partial.reshape(LAYERS, N_ROWS, rows, NX, cols).transpose(1, 3, 0, 2, 4)
    partial = partial.reshape(N_CHUNK, LAYERS, rows, cols)
    act = jnp.sum(lax.all_to_all(partial, CHUNK, 0, 0), axis=0)
    act = act + damp_act[:, None, None] * right.astype(jnp.float32)
    return act.astype(jnp.bfloat16)


def solution(mesh):
    fine = Mesh(mesh.devices.reshape(SIZES), AXES)
    return jax.shard_map(
        body,
        mesh=fine,
        in_specs=(
            P(None, BLK, OWNER),
            P(None, None, OWNER),
            P(OWNER, BLK, None),
            P(),
            P(),
            P(),
        ),
        out_specs=P(None, BLK, OWNER),
        check_vma=False,
    )
```

```python
import numpy as np
import jax
import jax.numpy as jnp
from jax import lax
from jax.experimental import pallas as pl
from jax.experimental.pallas import tpu as pltpu
from jax.sharding import Mesh, PartitionSpec as P

LAYERS = 2
AXES = ("za", "zb", "ya", "yb", "core", "yhi", "x")
SIZES = (6, 2, 2, 2, 2, 2, 4)
NX = 4
N_OWNER = 8
BLK = ("za", "zb", "ya", "yb", "core")
OWNER = ("yhi", "x")
CHUNK = ("zb", "yb", "x")
N_CHUNK = 16
N_ROWS = 4
BLOCKS = 6
FLIP = [(0, 1), (1, 0)]


def spread_pairs(flip):
    source = np.arange(np.prod(SIZES)).reshape(SIZES)
    pairs = []
    for za, zb, ya, yb, core, yhi, x in np.ndindex(*SIZES):
        target = source[za, zb, (x // 2) ^ flip, yb, x % 2, yhi, 2 * ya + core]
        pairs.append((int(source[za, zb, ya, yb, core, yhi, x]), int(target)))
    return pairs


def copies(value, axis, count):
    return lax.all_to_all(jnp.broadcast_to(value[None], (count,) + value.shape), axis, 0, 0)


def ordered(mine, other, axis):
    first = lax.axis_index(axis) == 0
    return jnp.stack([jnp.where(first, mine, other), jnp.where(first, other, mine)])


def chunk_kernel(factor_ref, chunks_ref):
    rows = factor_ref.shape[1]
    for zb, yb, ya, core in np.ndindex(2, 2, 2, 2):
        at = ((zb * 2 + ya) * 2 + yb) * 2 + core
        runs = [
            factor_ref[0, :, (za * N_CHUNK + at) * rows : (za * N_CHUNK + at + 1) * rows]
            for za in range(BLOCKS)
        ]
        chunks_ref[((zb * 2 + yb) * 2 + ya) * 2 + core] = jnp.concatenate(runs, axis=1)


def column_chunks(factor):
    _, rows, width = factor.shape
    return pl.pallas_call(
        chunk_kernel,
        out_shape=jax.ShapeDtypeStruct((N_CHUNK, rows, width // N_CHUNK), factor.dtype),
        cost_estimate=pl.CostEstimate(
            flops=0, bytes_accessed=4 * rows * width, transcendentals=0
        ),
    )(factor)


def product_kernel(choice, mine0, mine1, first, second, own, sibling, out_ref, factor):
    for layer, options in enumerate(((mine0, first), (mine1, first, second))):
        for at, option in enumerate(options):

            @pl.when(choice[layer] == at)
            def _():
                factor[layer] = option[...]

    rows, cols = out_ref.shape[2:]
    core = choice[LAYERS]
    for layer in range(LAYERS):
        columns = []
        for half in (own, sibling):
            for ya in range(2):
                part = half[:, ya, layer].astype(jnp.float32)
                columns.append(part.reshape(BLOCKS * rows, cols).astype(jnp.bfloat16))
        product = jnp.dot(
            factor[layer],
            jnp.concatenate(columns, axis=1),
            preferred_element_type=jnp.float32,
        )
        for block in range(N_ROWS):
            for at in range(NX):
                x = 2 * (at % 2) + (core if at < 2 else 1 - core)
                out_ref[block * NX + x, layer] = product[
                    block * rows : (block + 1) * rows, at * cols : (at + 1) * cols
                ]


def partial_products(choice, mine0, mine1, first, second, own, sibling):
    rows, cols = own.shape[3:]
    depth, width = mine0.shape
    vmem = pl.BlockSpec(memory_space=pltpu.VMEM)
    return pl.pallas_call(
        product_kernel,
        out_shape=jax.ShapeDtypeStruct((N_CHUNK, LAYERS, rows, cols), jnp.float32),
        in_specs=[pl.BlockSpec(memory_space=pltpu.SMEM)] + [vmem] * 6,
        out_specs=vmem,
        scratch_shapes=[pltpu.VMEM((LAYERS, depth, width), jnp.bfloat16)],
        cost_estimate=pl.CostEstimate(
            flops=2 * LAYERS * depth * width * NX * cols,
            bytes_accessed=8 * depth * width + 4 * own.size + 4 * N_CHUNK * LAYERS * rows * cols,
            transcendentals=0,
        ),
    )(choice, mine0, mine1, first, second, own, sibling)


def body(grad_blocks, ginv_factors, ainv_owned, owner_table, damp_grad, damp_act):
    rows, cols = grad_blocks.shape[1:]
    width = ainv_owned.shape[2] // N_CHUNK
    yhi = lax.axis_index("yhi")

    gathered = copies(grad_blocks, OWNER, N_OWNER)
    gathered = gathered.transpose(1, 2, 0, 3).reshape(LAYERS, rows, N_OWNER * cols)
    right = lax.dot_general(
        gathered, ginv_factors, (((2,), (1,)), ((0,), (0,))), preferred_element_type=jnp.float32
    )
    right = right + damp_grad[:, None, None] * grad_blocks.astype(jnp.float32)
    right = right.astype(jnp.bfloat16)
    near = lax.ppermute(right, AXES, spread_pairs(0))
    far = lax.ppermute(right, AXES, spread_pairs(1))
    piece = ordered(near, far, "ya")

    factor = column_chunks(ainv_owned)
    factor = lax.all_to_all(factor, CHUNK, 0, 0).reshape(N_ROWS, NX, rows, width)
    owner_half = owner_table // NX
    here = owner_half == yhi

    def of_owner(owner):
        part = lax.dynamic_index_in_dim(factor, owner % NX, 1, keepdims=False)
        return part.reshape(N_ROWS * rows, width)

    mine = [of_owner(owner_table[l]) for l in range(LAYERS)]
    one_half = owner_half[0] == owner_half[1]
    first = of_owner(jnp.where(here[0], owner_table[0], owner_table[1]))
    first, piece = lax.optimization_barrier((first, piece))
    first = lax.ppermute(first, "yhi", FLIP)
    second = lax.cond(one_half, lambda part: lax.ppermute(part, "yhi", FLIP), lambda part: part, mine[1])

    along = copies(piece, "za", BLOCKS)
    damped = damp_act[:, None, None] * right.astype(jnp.float32)
    choice = jnp.stack(
        [
            jnp.where(here[0], 0, 1),
            jnp.where(here[1], 0, jnp.where(one_half, 2, 1)),
            lax.axis_index("core"),
        ]
    ).astype(jnp.int32)
    along, first, second, damped, choice = lax.optimization_barrier(
        (along, first, second, damped, choice)
    )
    sibling = lax.ppermute(along, "core", FLIP)
    partial = partial_products(choice, mine[0], mine[1], first, second, along, sibling)
    act = jnp.sum(lax.all_to_all(partial, CHUNK, 0, 0), axis=0)
    return (act + damped).astype(jnp.bfloat16)


def solution(mesh):
    fine = Mesh(mesh.devices.reshape(SIZES), AXES)
    return jax.shard_map(
        body,
        mesh=fine,
        in_specs=(
            P(None, BLK, OWNER),
            P(None, None, OWNER),
            P(OWNER, BLK, None),
            P(),
            P(),
            P(),
        ),
        out_specs=P(None, BLK, OWNER),
        check_vma=False,
    )
```

```python
import numpy as np
import jax
import jax.numpy as jnp
from jax import lax
from jax.experimental import pallas as pl
from jax.sharding import Mesh, PartitionSpec as P

LAYERS = 2
AXES = ("za", "zb", "ya", "yb", "core", "yhi", "x")
SIZES = (6, 2, 2, 2, 2, 2, 4)
NX = 4
N_OWNER = 8
BLK = ("za", "zb", "ya", "yb", "core")
OWNER = ("yhi", "x")
CHUNK = ("zb", "yb", "x")
N_CHUNK = 16
N_ROWS = 4
BLOCKS = 6
FLIP = [(0, 1), (1, 0)]


def spread_pairs(flip):
    source = np.arange(np.prod(SIZES)).reshape(SIZES)
    pairs = []
    for za, zb, ya, yb, core, yhi, x in np.ndindex(*SIZES):
        target = source[za, zb, (x // 2) ^ flip, yb, x % 2, yhi, 2 * ya + core]
        pairs.append((int(source[za, zb, ya, yb, core, yhi, x]), int(target)))
    return pairs


def copies(value, axis, count):
    return lax.all_to_all(jnp.broadcast_to(value[None], (count,) + value.shape), axis, 0, 0)


def ordered(mine, other, axis):
    first = lax.axis_index(axis) == 0
    return jnp.stack([jnp.where(first, mine, other), jnp.where(first, other, mine)])


def chunk_kernel(factor_ref, chunks_ref):
    rows = factor_ref.shape[1]
    for zb, yb, ya, core in np.ndindex(2, 2, 2, 2):
        at = ((zb * 2 + ya) * 2 + yb) * 2 + core
        runs = [
            factor_ref[0, :, (za * N_CHUNK + at) * rows : (za * N_CHUNK + at + 1) * rows]
            for za in range(BLOCKS)
        ]
        chunks_ref[((zb * 2 + yb) * 2 + ya) * 2 + core] = jnp.concatenate(runs, axis=1)


def column_chunks(factor):
    _, rows, width = factor.shape
    return pl.pallas_call(
        chunk_kernel,
        out_shape=jax.ShapeDtypeStruct((N_CHUNK, rows, width // N_CHUNK), factor.dtype),
        cost_estimate=pl.CostEstimate(
            flops=0, bytes_accessed=4 * rows * width, transcendentals=0
        ),
    )(factor)


def body(grad_blocks, ginv_factors, ainv_owned, owner_table, damp_grad, damp_act):
    rows, cols = grad_blocks.shape[1:]
    width = ainv_owned.shape[2] // N_CHUNK
    yhi = lax.axis_index("yhi")

    gathered = copies(grad_blocks, OWNER, N_OWNER)
    gathered = gathered.transpose(1, 2, 0, 3).reshape(LAYERS, rows, N_OWNER * cols)
    right = lax.dot_general(
        gathered, ginv_factors, (((2,), (1,)), ((0,), (0,))), preferred_element_type=jnp.float32
    )
    right = right + damp_grad[:, None, None] * grad_blocks.astype(jnp.float32)
    right = right.astype(jnp.bfloat16)
    near = lax.ppermute(right, AXES, spread_pairs(0))
    far = lax.ppermute(right, AXES, spread_pairs(1))
    piece = ordered(near, far, "ya")

    factor = column_chunks(ainv_owned)
    factor = lax.all_to_all(factor, CHUNK, 0, 0).reshape(N_ROWS, NX, rows, width)
    owner_half = owner_table // NX
    here = owner_half == yhi

    def of_owner(owner):
        part = lax.dynamic_index_in_dim(factor, owner % NX, 1, keepdims=False)
        return part.reshape(N_ROWS * rows, width)

    mine = [of_owner(owner_table[l]) for l in range(LAYERS)]
    one_half = owner_half[0] == owner_half[1]
    first = of_owner(jnp.where(here[0], owner_table[0], owner_table[1]))
    first, piece = lax.optimization_barrier((first, piece))
    first = lax.ppermute(first, "yhi", FLIP)
    second = lax.cond(one_half, lambda part: lax.ppermute(part, "yhi", FLIP), lambda part: part, mine[1])

    along = lax.all_gather(piece, "za")
    along, first, second = lax.optimization_barrier((along, first, second))
    factor = jnp.stack(
        [
            jnp.where(here[0], mine[0], first),
            jnp.where(here[1], mine[1], jnp.where(one_half, second, first)),
        ]
    )
    chunk = ordered(along, lax.ppermute(along, "core", FLIP), "core")
    chunk = chunk.transpose(3, 1, 4, 2, 0, 5).reshape(LAYERS, BLOCKS * rows, NX * cols)

    partial = lax.dot_general(
        factor, chunk, (((2,), (1,)), ((0,), (0,))), preferred_element_type=jnp.float32
    )
    partial = partial.reshape(LAYERS, N_ROWS, rows, NX, cols).transpose(1, 3, 0, 2, 4)
    partial = partial.reshape(N_CHUNK, LAYERS, rows, cols)
    act = jnp.sum(lax.all_to_all(partial, CHUNK, 0, 0), axis=0)
    act = act + damp_act[:, None, None] * right.astype(jnp.float32)
    return act.astype(jnp.bfloat16)


def solution(mesh):
    fine = Mesh(mesh.devices.reshape(SIZES), AXES)
    return jax.shard_map(
        body,
        mesh=fine,
        in_specs=(
            P(None, BLK, OWNER),
            P(None, None, OWNER),
            P(OWNER, BLK, None),
            P(),
            P(),
            P(),
        ),
        out_specs=P(None, BLK, OWNER),
        check_vma=False,
    )
```
